512 devices in a mesh: row: 16 (over z_lo, x), col: 32 (over z_hi, y, core).
Axes of the slice: x: 4, y: 8, z: 8 (z_hi: 2, z_lo: 4; z = z_hi * 4 + z_lo), core: 2. Of those that a mesh axis runs over, the one named last changes fastest.
Arguments:
- front: float32 [4, 4096, 2, 8192], P(None, 'row', None, 'col'), may hold values from -6 to 6
- contrib: float32 [1, 4096, 1, 8192], P(None, 'row', None, 'col'), may hold values from -6 to 6
- child_map: int32 [2, 16], replicated, may hold values from 0 to 63, as said below
- pattern: int32 [2, 16, 16], replicated, may hold values 0 or 1
- inverse: float32 [1024, 1024], P('col'), as said below
Outputs:
- updated: float32 [4, 4096, 2, 8192], P(None, 'row', None, 'col')
The draws below stay inside these ranges and needn't reach their ends.
Inputs may be any that keep to these rules, and one draw needn't show every extreme that they name: Each row of child_map (each child) holds 16 distinct parent blocks, and child_map[h, a] leaves the same remainder modulo 16 as a. `inverse`: lower triangular with a positive diagonal.
All inputs are finite; a program needn't handle non-finite values.
Results may differ from the reference program's by a relative error of at most 0.000098.
Values sent between devices are 32-bit elements; how exact they have to be, the bound alone decides.
A program may use at most 64 MiB of HBM per device.

```python
import jax
import jax.numpy as jnp
from jax import lax

BLK = 256
FRONT = 16384
PANEL = 1024
CHILD = 4096
BLOCKS = 64
CHILD_BLOCKS = 16
ROW_SLOTS = 4
COL_SLOTS = 2
CHILD_SLOTS = 1
N_ROW = 16
N_COL = 32


def draw_child_map(key, part):
    key = jax.random.fold_in(key, 11)
    option_count = BLOCKS // N_ROW
    take_count = CHILD_BLOCKS // N_ROW
    scores = jax.random.randint(key, (2, N_ROW, option_count), 0, 1 << 20) * option_count + jnp.arange(option_count)
    scores = scores.at[0, N_ROW - 1, option_count - 1].set(-1).at[1, 0, 0].set(-1)
    ranking = jnp.argsort(scores, axis=-1)
    picked = ranking[:, :, :take_count]
    residues = jnp.arange(N_ROW)[None, :, None]
    values = residues + N_ROW * picked
    return values.transpose(0, 2, 1).reshape(2, CHILD_BLOCKS).astype(jnp.int32)


def draw_inverse(key, part):
    key = jax.random.fold_in(key, 5)
    noise_key, diag_key = jax.random.split(key)
    row_ids = jnp.arange(PANEL, dtype=jnp.float32)[:, None]
    col_ids = jnp.arange(PANEL, dtype=jnp.float32)[None, :]
    noise = jax.random.normal(noise_key, (PANEL, PANEL), jnp.float32)
    diagonal = jax.random.uniform(diag_key, (PANEL, 1), jnp.float32, 0.7, 1.4)
    scale = PANEL ** (-0.25)
    lower = jnp.where(col_ids < row_ids, noise * scale / jnp.sqrt(row_ids + 1.0), 0.0)
    return (lower + jnp.where(col_ids == row_ids, diagonal * scale, 0.0)).astype(jnp.float32)


def set_ends(values, rng, smallest, largest):
    longest = values.shape.index(max(values.shape))
    spots = []
    for shift in (0, 1):
        where = [jax.random.randint(jax.random.fold_in(rng, axis), (), 0, length) for axis, length in enumerate(values.shape)]
        where[longest] = (where[longest] + shift) % values.shape[longest]
        spots.append(tuple(where))
    return values.at[spots[0]].set(smallest).at[spots[1]].set(largest)


def steps_of(rng, extent, shards, smallest, top_value):
    loudness = 1.0
    for position, shards_of in shards:
        heights = jax.random.uniform(jax.random.fold_in(jax.random.fold_in(rng, 6), position), (shards_of,), jnp.float32, smallest / len(shards), top_value / len(shards))
        loudness = loudness * jnp.repeat(jnp.exp(heights), extent[position] // shards_of).reshape((-1,) + (1,) * (len(extent) - 1 - position))
    return loudness


def centred(own_key, extent, width, most, cuts=(), held_as=jnp.bfloat16):
    values = jax.random.normal(own_key, extent, jnp.float32) * width
    if len(cuts) > 0:
        values = steps_of(own_key, extent, cuts, -0.22, 0.18) * values
    return jnp.clip(values, min=-most, max=most).astype(held_as)


def setup_inputs(seed: int = 0) -> dict:
    key_list = jax.random.split(jax.random.key(seed), 6)
    front = centred(key_list[0], (ROW_SLOTS, N_ROW * BLK, COL_SLOTS, N_COL * BLK), 1.0, 6.0, ((1, 16), (3, 32)), jnp.float32)
    contrib = centred(key_list[1], (CHILD_SLOTS, N_ROW * BLK, CHILD_SLOTS, N_COL * BLK), 1.0, 6.0, ((1, 16), (3, 32)), jnp.float32)
    child_map = draw_child_map(jax.random.fold_in(key_list[5], 71), 0)
    pattern = set_ends((jax.random.randint(key_list[3], (2, CHILD_BLOCKS, CHILD_BLOCKS), 0, 4) < 3).astype(jnp.int32), jax.random.fold_in(key_list[3], 1), 0, 1)
    inverse = draw_inverse(jax.random.fold_in(key_list[5], 71), 0)
    return dict(front=front, contrib=contrib, child_map=child_map, pattern=pattern, inverse=inverse)


def reference(front, contrib, child_map, pattern, inverse):
    block_count = FRONT // BLK
    child_count = CHILD // BLK
    child_slots = child_count // N_ROW
    half_count = N_COL // 2
    children = contrib.reshape(child_slots, N_ROW, BLK, child_slots, 2, half_count, BLK)
    children = children.transpose(4, 0, 1, 2, 3, 5, 6).reshape(2, child_count, BLK, child_count, BLK)
    tiles = front.reshape(block_count, BLK, block_count, BLK)
    for child_index in range(2):
        parents = child_map[child_index].astype(jnp.int32)
        weights = pattern[child_index].astype(jnp.float32)
        values = children[child_index] * weights[:, None, :, None]
        tiles = tiles.at[parents[:, None], :, parents[None, :], :].add(values.transpose(0, 2, 1, 3))
    assembled = tiles.reshape(FRONT, FRONT)
    factor = jnp.dot(assembled[:, :PANEL], inverse.T, precision=lax.Precision.HIGHEST)
    tail_rows = factor[PANEL:]
    trailing = assembled[PANEL:, PANEL:] - jnp.dot(tail_rows, tail_rows.T, precision=lax.Precision.HIGHEST)
    result = assembled.at[:, :PANEL].set(factor).at[PANEL:, PANEL:].set(trailing)
    return result.reshape(block_count // N_ROW, N_ROW * BLK, block_count // N_COL, N_COL * BLK)
```

```python
import functools

import jax
import jax.numpy as jnp
from jax import lax
from jax.experimental import pallas as pl
from jax.experimental.pallas import tpu as pltpu
from jax.sharding import PartitionSpec as P

MESH = pl.DeviceIdType.MESH
F32 = jnp.float32
BF16 = jnp.bfloat16

BLK = 256
ROWS = 1024
CH = 64
NCH = ROWS // CH
PER_SLOT = BLK // CH
HOP_NUM, HOP_DEN = 5, 2
R_OFF = 3
GRP = 128
MAX_HOPS = 14
STEPS = NCH + (MAX_HOPS * HOP_NUM) // HOP_DEN + R_OFF + 1


def nt_dot(a, b):
    return lax.dot_general(a, b, (((1,), (1,)), ((), ())), preferred_element_type=F32)


def split(x):
    hi = x.astype(BF16)
    return hi, (x - hi.astype(F32)).astype(BF16)


def kernel(
    front, contrib, cmap, pattern, inv, out,
    fac, facc, pan, cpart, invx, wbuf, wh, wl, fh, fl, ch, cl,
    r_recv, c_recv, a_recv, w_recv, x_recv,
    fwd_s, rev_s, cross_s, sib_s, c_s, a_s, w_s, x_s,
):
    r = lax.axis_index("row")
    c = lax.axis_index("col")
    x, zlo = lax.rem(r, 4), r // 4
    zhi, y, core = c // 16, lax.rem(c // 2, 8), lax.rem(c, 2)
    n0 = lax.rem(c, 16) // 8

    def dev(x_, zlo_, zhi_, y_, core_):
        return (zlo_ * 4 + x_, zhi_ * 16 + y_ * 2 + core_)

    y_up = dev(x, zlo, zhi, lax.rem(y + 1, 8), core)
    y_dn = dev(x, zlo, zhi, lax.rem(y + 7, 8), core)
    sib = dev(x, zlo, zhi, y, 1 - core)
    part = dev(x, zlo, 1 - zhi, y, core)
    x_up = dev(lax.rem(x + 1, 4), zlo, zhi, y, core)
    x_dn = dev(lax.rem(x + 3, 4), zlo, zhi, y, core)
    z_up = dev(x, jnp.minimum(zlo + 1, 3), zhi, y, core)
    z_dn = dev(x, jnp.maximum(zlo - 1, 0), zhi, y, core)
    panel_dev = (zhi == 0) & (y < 2)

    def remote(src, dst, ss, rs, to):
        return pltpu.make_async_remote_copy(
            src_ref=src, dst_ref=dst, send_sem=ss, recv_sem=rs, device_id=to, device_id_type=MESH
        )

    def landed(ref, sem):
        pltpu.make_async_copy(ref, ref, sem).wait()

    bar = pltpu.get_barrier_semaphore()

    def greet(to):
        pl.semaphore_signal(bar, inc=1, device_id=to, device_id_type=MESH)

    for to in (y_up, y_dn, sib, part, x_up, x_dn):
        greet(to)

    @pl.when(zlo < 3)
    def _():
        greet(z_up)

    @pl.when(zlo > 0)
    def _():
        greet(z_dn)

    @pl.when(panel_dev)
    def _():
        def one(p, carry):
            peer = lax.rem(c, 2) * 8 + p

            @pl.when(peer != c)
            def _():
                greet((r, peer))

            return carry

        lax.fori_loop(0, 8, one, 0)

    expect = 6 + (zlo < 3).astype(jnp.int32) + (zlo > 0).astype(jnp.int32)
    from_panel = (n0 != c).astype(jnp.int32) + (n0 + 2 != c).astype(jnp.int32)
    expect = expect + jnp.where(zhi == 0, from_panel, 0)
    pl.semaphore_wait(bar, expect)

    child_copy = remote(contrib, cpart, x_s.at[0], x_recv.at[0], part)
    inv_copy = remote(inv, invx, x_s.at[1], x_recv.at[1], part)
    wrow = pl.ds(pl.multiple_of(lax.rem(c, 8) * 32, 32), 32)
    wslot = lax.rem(c, 8)

    def inverse_rows(src, which, owner, wait):
        for k in range(4):
            cols = pl.ds(k * BLK, BLK)

            @pl.when(k <= owner)
            def _(k=k, cols=cols):
                @pl.when(owner == c)
                def _():
                    if not wait:
                        wbuf[wrow, cols] = src[:, cols]

                @pl.when(owner != c)
                def _():
                    cp = remote(
                        src.at[:, cols], wbuf.at[wrow, cols],
                        w_s.at[which * 4 + k], w_recv.at[wslot * 4 + k], (r, owner),
                    )
                    if wait:
                        cp.wait_send()
                    else:
                        cp.start()

    @pl.when(zhi == 1)
    def _():
        @pl.when(y < 2)
        def _():
            child_copy.start()
            inv_copy.start()

        @pl.when(y >= 2)
        def _():
            inv_copy.start()
            child_copy.start()

    @pl.when(zhi == 0)
    def _():
        inverse_rows(inv, 0, n0, False)
        landed(invx, x_recv.at[1])
        inverse_rows(invx, 1, n0 + 2, False)

        @pl.when(y >= 2)
        def _():
            child_copy.start()

    scol = lax.rem(c, 16)

    def weight(h, i, j):
        hit = (cmap[h, r] == i * 16 + r) & (cmap[h, scol] == j * 32 + c)
        return jnp.where(hit, pattern[h * 16 + r, scol], 0).astype(F32)

    def base(i, j):
        return (
            front[i * 2 + j]
            + weight(zhi, i, j) * contrib[...]
            + weight(1 - zhi, i, j) * cpart[...]
        )

    def grp_rows(g):
        return pl.ds(pl.multiple_of(g * GRP, GRP), GRP)

    def pan_copy(k, g, kind, to):
        part_ref = pan.at[k, grp_rows(g)]
        return remote(part_ref, part_ref, a_s.at[kind], a_recv.at[k * 8 + g], to)

    @pl.when(panel_dev)
    def _():
        landed(cpart, x_recv.at[0])
        child_copy.start()
        for i in range(4):
            pan[c, pl.ds(i * BLK, BLK)] = base(i, 0)

        def send_all(to, kind):
            def one(g, carry):
                pan_copy(c, g, kind, to).start()
                return carry

            lax.fori_loop(0, 8, one, 0)

        @pl.when(y == 0)
        def _():
            send_all(y_up, 0)

        @pl.when(core == 0)
        def _():
            send_all(sib, 1)

        def piece(p, carry):
            for k in range(4):
                @pl.when((k <= c) & (lax.rem(c, 2) * 8 + p != c))
                def _(k=k):
                    landed(
                        wbuf.at[pl.ds(pl.multiple_of(p * 32, 32), 32), pl.ds(k * BLK, BLK)],
                        w_recv.at[p * 4 + k],
                    )

            return carry

        lax.fori_loop(0, 8, piece, 0)
        for k in range(4):
            @pl.when(k <= c)
            def _(k=k):
                hi, lo = split(wbuf[:, pl.ds(k * BLK, BLK)])
                wh[k] = hi
                wl[k] = lo

    def make_factor(g):
        @pl.when(y == 1)
        def _():
            @pl.when(core == 0)
            def _():
                landed(pan.at[0, grp_rows(g)], a_recv.at[g])
                pan_copy(0, g, 2, sib).start()
                landed(pan.at[1, grp_rows(g)], a_recv.at[8 + g])

            @pl.when(core == 1)
            def _():
                landed(pan.at[1, grp_rows(g)], a_recv.at[8 + g])
                pan_copy(1, g, 2, sib).start()
                landed(pan.at[0, grp_rows(g)], a_recv.at[g])
                landed(pan.at[2, grp_rows(g)], a_recv.at[16 + g])

        @pl.when((y == 0) & (core == 1))
        def _():
            landed(pan.at[0, grp_rows(g)], a_recv.at[g])

        def add(k, acc):
            ah, al = split(pan[k, grp_rows(g)])
            return acc + nt_dot(ah, wh[k]) + (nt_dot(ah, wl[k]) + nt_dot(al, wh[k]))

        fac[c, grp_rows(g)] = lax.fori_loop(0, c + 1, add, jnp.zeros((GRP, BLK), F32))

    xs = 2 * lax.rem(y, 2) + core
    zs = y // 2
    dxs = lax.rem(x - xs + 4, 4)
    dz = jnp.abs(zlo - zs)
    c_dist = dz + jnp.where(dxs == 3, 1, dxs)
    c_go = (
        ((zlo >= zs) & (zlo < 3) & (dxs == 0), z_up),
        ((zlo <= zs) & (zlo > 0) & (dxs == 0), z_dn),
        ((dxs == 0) | ((core == 1) & (dxs == 1)), x_up),
        ((dxs == 0) | ((core == 0) & (dxs == 3)), x_dn),
    )

    def position(s):
        return jnp.where(s == 0, lax.rem(8 - y, 8), lax.rem(y + 7, 8))

    def lag(hops, s):
        return (hops * HOP_NUM) // HOP_DEN + s * R_OFF

    def ch_rows(m):
        return pl.ds(pl.multiple_of(m * CH, CH), CH)

    def step(t, carry):
        @pl.when(panel_dev & (lax.rem(t - y * R_OFF + 16, 2) == 0) & (t >= y * R_OFF) & (t < NCH + y * R_OFF))
        def _():
            make_factor((t - y * R_OFF) // 2)

        def stream(sq, carry):
            s, q = sq // 4, lax.rem(sq, 4)
            pos = position(s)
            d = lax.rem(pos - q + 8, 8)
            hops = jnp.where(zhi == 0, pos, q + 1 + jnp.where(d <= 4, d, 8 - d))
            go_fwd = jnp.where(zhi == 0, pos < 7, d <= 3)
            go_rev = (zhi == 1) & ((d == 0) | (d >= 6))
            go_cross = (zhi == 0) & (pos == q)
            first = (zhi == 0) & (pos == 0)
            own, other = 2 * s + core, 2 * s + 1 - core

            def chunk_now(extra):
                m = t - lag(hops + extra, s)
                return m, (m >= 0) & (m < NCH) & (lax.rem(m + 64, 4) == q)

            m, now = chunk_now(0)

            @pl.when(now)
            def _():
                ref = fac.at[own, ch_rows(m)]
                sem = r_recv.at[own * NCH + m]

                @pl.when(jnp.logical_not(first))
                def _():
                    landed(ref, sem)

                @pl.when(go_fwd & (s == 0))
                def _():
                    remote(ref, ref, fwd_s.at[sq], sem, y_dn).start()

                @pl.when(go_fwd & (s == 1))
                def _():
                    remote(ref, ref, fwd_s.at[sq], sem, y_up).start()

                @pl.when(go_rev & (s == 0))
                def _():
                    remote(ref, ref, rev_s.at[sq], sem, y_up).start()

                @pl.when(go_rev & (s == 1))
                def _():
                    remote(ref, ref, rev_s.at[sq], sem, y_dn).start()

                @pl.when(go_cross)
                def _():
                    remote(ref, ref, cross_s.at[sq], sem, part).start()

                remote(ref, ref, sib_s.at[sq], sem, sib).start()

            m1, now1 = chunk_now(1)

            @pl.when(now1)
            def _():
                landed(fac.at[other, ch_rows(m1)], r_recv.at[other * NCH + m1])

            for n, extra in ((own, 0), (other, 1)):
                mc, nowc = chunk_now(extra + c_dist)
                slot = mc // PER_SLOT

                @pl.when(nowc & (lax.rem(slot, 2) == zhi))
                def _(n=n, mc=mc, slot=slot):
                    idx = (slot // 2) * PER_SLOT + lax.rem(mc, PER_SLOT)
                    dst = facc.at[n, ch_rows(idx)]
                    sem = c_recv.at[n * (NCH // 2) + idx]

                    @pl.when(c_dist == 0)
                    def _():
                        src = fac.at[n, ch_rows(mc)]
                        for kind, (go, to) in enumerate(c_go):
                            @pl.when(go)
                            def _(kind=kind, to=to):
                                remote(src, dst, c_s.at[kind * 4 + n], sem, to).start()

                    @pl.when(c_dist > 0)
                    def _():
                        landed(dst, sem)
                        for kind, (go, to) in enumerate(c_go):
                            @pl.when(go)
                            def _(kind=kind, to=to):
                                remote(dst, dst, c_s.at[kind * 4 + n], sem, to).start()

            return carry

        return lax.fori_loop(0, 8, stream, carry)

    lax.fori_loop(0, STEPS, step, 0)

    @pl.when(jnp.logical_not(panel_dev))
    def _():
        landed(cpart, x_recv.at[0])

    for n in range(4):
        cols = pl.ds(n * BLK, BLK)
        for i in range(4):
            rows = pl.ds(i * BLK, BLK)
            hi, lo = split(fac[n, rows])
            fh[rows, cols] = hi
            fl[rows, cols] = lo
        for j in range(2):
            rows = pl.ds(j * BLK, BLK)

            @pl.when(c_dist == 0)
            def _(n=n, j=j, rows=rows, cols=cols):
                at = pl.multiple_of((2 * j + zhi) * BLK, BLK)
                hi, lo = split(fac[n, pl.ds(at, BLK)])
                ch[rows, cols] = hi
                cl[rows, cols] = lo

            @pl.when(c_dist > 0)
            def _(n=n, j=j, rows=rows, cols=cols):
                hi, lo = split(facc[n, rows])
                ch[rows, cols] = hi
                cl[rows, cols] = lo

    def update(i, carry):
        rows = pl.ds(pl.multiple_of(i * BLK, BLK), BLK)
        for j in range(2):
            def trail(j=j):
                cr = pl.ds(j * BLK, BLK)
                u = nt_dot(fh[rows], ch[cr]) + (nt_dot(fh[rows], cl[cr]) + nt_dot(fl[rows], ch[cr]))
                on = ((i * 16 + r >= 4) & (j * 32 + c >= 4)).astype(jnp.int32).astype(F32)
                out[i * 2 + j] = base(i, j) - on * u

            if j == 0:
                pl.when(c >= 4)(trail)

                @pl.when(c < 4)
                def _():
                    out[i * 2] = fac[jnp.minimum(c, 3), rows]
            else:
                trail()
        return carry

    lax.fori_loop(0, 4, update, 0)

    def left(ref, sem):
        remote(ref, ref, sem, sem, sib).wait_send()

    def sent(sq, carry):
        s, q = sq // 4, lax.rem(sq, 4)
        pos = position(s)
        d = lax.rem(pos - q + 8, 8)
        quarter = fac.at[0, pl.ds(0, ROWS // 4)]

        @pl.when(jnp.where(zhi == 0, pos < 7, d <= 3))
        def _():
            left(quarter, fwd_s.at[sq])

        @pl.when((zhi == 1) & ((d == 0) | (d >= 6)))
        def _():
            left(quarter, rev_s.at[sq])

        @pl.when((zhi == 0) & (pos == q))
        def _():
            left(quarter, cross_s.at[sq])

        left(quarter, sib_s.at[sq])
        return carry

    lax.fori_loop(0, 8, sent, 0)
    for kind, (go, _to) in enumerate(c_go):
        for n in range(4):
            @pl.when(go)
            def _(kind=kind, n=n):
                left(facc.at[n], c_s.at[kind * 4 + n])

    child_copy.wait_send()

    @pl.when(zhi == 1)
    def _():
        inv_copy.wait_send()

    @pl.when(zhi == 0)
    def _():
        inverse_rows(inv, 0, n0, True)
        inverse_rows(invx, 1, n0 + 2, True)

    @pl.when(panel_dev)
    def _():
        @pl.when(y == 0)
        def _():
            left(pan.at[0], a_s.at[0])

        @pl.when(core == 0)
        def _():
            left(pan.at[0], a_s.at[1])

        @pl.when(y == 1)
        def _():
            left(pan.at[0], a_s.at[2])


def body(front, contrib, child_map, pattern, inverse):
    vm = pl.BlockSpec(memory_space=pltpu.VMEM)
    sm = pl.BlockSpec(memory_space=pltpu.SMEM)
    dma = pltpu.SemaphoreType.DMA
    front_t = front.transpose(0, 2, 1, 3).reshape(8, BLK, BLK)
    out = pl.pallas_call(
        kernel,
        out_shape=jax.ShapeDtypeStruct((8, BLK, BLK), F32),
        in_specs=[vm, vm, sm, sm, vm],
        out_specs=vm,
        scratch_shapes=[
            pltpu.VMEM((4, ROWS, BLK), F32),
            pltpu.VMEM((4, ROWS // 2, BLK), F32),
            pltpu.VMEM((4, ROWS, BLK), F32),
            pltpu.VMEM((BLK, BLK), F32),
            pltpu.VMEM((32, 1024), F32),
            pltpu.VMEM((BLK, 1024), F32),
            pltpu.VMEM((4, BLK, BLK), BF16),
            pltpu.VMEM((4, BLK, BLK), BF16),
            pltpu.VMEM((ROWS, 1024), BF16),
            pltpu.VMEM((ROWS, 1024), BF16),
            pltpu.VMEM((ROWS // 2, 1024), BF16),
            pltpu.VMEM((ROWS // 2, 1024), BF16),
            dma((4 * NCH,)),
            dma((4 * NCH // 2,)),
            dma((32,)),
            dma((32,)),
            dma((2,)),
            dma((8,)),
            dma((8,)),
            dma((8,)),
            dma((8,)),
            dma((16,)),
            dma((3,)),
            dma((8,)),
            dma((2,)),
        ],
        compiler_params=pltpu.CompilerParams(
            collective_id=0, has_side_effects=True, vmem_limit_bytes=48 << 20
        ),
        name="panel_step",
    )(front_t, contrib.reshape(BLK, BLK), child_map, pattern.reshape(32, 16), inverse)
    return out.reshape(4, 2, BLK, BLK).transpose(0, 2, 1, 3)


def solution(mesh):
    return jax.shard_map(
        body,
        mesh=mesh,
        in_specs=(
            P(None, "row", None, "col"),
            P(None, "row", None, "col"),
            P(),
            P(),
            P("col", None),
        ),
        out_specs=P(None, "row", None, "col"),
        check_vma=False,
    )
```

```python
import functools

import jax
import jax.numpy as jnp
from jax import lax
from jax.experimental import pallas as pl
from jax.experimental.pallas import tpu as pltpu
from jax.sharding import PartitionSpec as P

MESH = pl.DeviceIdType.MESH
F32 = jnp.float32
BF16 = jnp.bfloat16

BLK = 256
ROWS = 1024
CH = 64
NCH = ROWS // CH
PER_SLOT = BLK // CH
HOP_NUM, HOP_DEN = 3, 1
R_OFF = 1
GRP = 128
PER_GRP = GRP // CH
C_SLACK = 0
AHEAD = 2


def nt_dot(a, b):
    return lax.dot_general(a, b, (((1,), (1,)), ((), ())), preferred_element_type=F32)


def split(x):
    hi = x.astype(BF16)
    return hi, (x - hi.astype(F32)).astype(BF16)


def kernel(
    front, contrib, cmap, pattern, inv, out,
    fac, facc, pan, cpart, invx, wbuf, wh, wl, fh, fl, ch, cl,
    r_recv, c_recv, a_recv, w_recv, x_recv,
    fwd_s, rev_s, cross_s, sib_s, c_s, a_s, w_s, x_s,
):
    r = lax.axis_index("row")
    c = lax.axis_index("col")
    x, zlo = lax.rem(r, 4), r // 4
    zhi, y, core = c // 16, lax.rem(c // 2, 8), lax.rem(c, 2)
    n0 = lax.rem(c, 16) // 8

    def dev(x_, zlo_, zhi_, y_, core_):
        return (zlo_ * 4 + x_, zhi_ * 16 + y_ * 2 + core_)

    y_up = dev(x, zlo, zhi, lax.rem(y + 1, 8), core)
    y_dn = dev(x, zlo, zhi, lax.rem(y + 7, 8), core)
    sib = dev(x, zlo, zhi, y, 1 - core)
    part = dev(x, zlo, 1 - zhi, y, core)
    mirror = dev(x, 3 - zlo, 1 - zhi, y, core)
    x_up = dev(lax.rem(x + 1, 4), zlo, zhi, y, core)
    x_dn = dev(lax.rem(x + 3, 4), zlo, zhi, y, core)
    z_up = dev(x, jnp.minimum(zlo + 1, 3), zhi, y, core)
    z_dn = dev(x, jnp.maximum(zlo - 1, 0), zhi, y, core)
    panel_dev = (zhi == 0) & (y < 2)

    def remote(src, dst, ss, rs, to):
        return pltpu.make_async_remote_copy(
            src_ref=src, dst_ref=dst, send_sem=ss, recv_sem=rs, device_id=to, device_id_type=MESH
        )

    def landed(ref, sem):
        pltpu.make_async_copy(ref, ref, sem).wait()

    bar = pltpu.get_barrier_semaphore()

    def greet(to):
        pl.semaphore_signal(bar, inc=1, device_id=to, device_id_type=MESH)

    for to in (y_up, y_dn, sib, part, mirror, x_up, x_dn):
        greet(to)

    @pl.when(zlo < 3)
    def _():
        greet(z_up)

    @pl.when(zlo > 0)
    def _():
        greet(z_dn)

    @pl.when(panel_dev)
    def _():
        def one(p, carry):
            peer = lax.rem(c, 2) * 8 + p

            @pl.when(peer != c)
            def _():
                greet((r, peer))

            return carry

        lax.fori_loop(0, 8, one, 0)

    expect = 7 + (zlo < 3).astype(jnp.int32) + (zlo > 0).astype(jnp.int32)
    from_panel = (n0 != c).astype(jnp.int32) + (n0 + 2 != c).astype(jnp.int32)
    expect = expect + jnp.where(zhi == 0, from_panel, 0)
    pl.semaphore_wait(bar, expect)

    child_copy = remote(contrib, cpart, x_s.at[0], x_recv.at[0], part)
    inv_copy = remote(inv, invx, x_s.at[1], x_recv.at[1], mirror)
    wrow = pl.ds(pl.multiple_of(lax.rem(c, 8) * 32, 32), 32)
    wslot = lax.rem(c, 8)

    def inverse_rows(src, which, owner, wait):
        for k in range(4):
            cols = pl.ds(k * BLK, BLK)

            @pl.when(k <= owner)
            def _(k=k, cols=cols):
                @pl.when(owner == c)
                def _():
                    if not wait:
                        wbuf[wrow, cols] = src[:, cols]

                @pl.when(owner != c)
                def _():
                    cp = remote(
                        src.at[:, cols], wbuf.at[wrow, cols],
                        w_s.at[which * 4 + k], w_recv.at[wslot * 4 + k], (r, owner),
                    )
                    if wait:
                        cp.wait_send()
                    else:
                        cp.start()

    @pl.when(zhi == 1)
    def _():
        @pl.when(y < 2)
        def _():
            child_copy.start()
            inv_copy.start()
            inv_copy.wait_send()

        @pl.when(y >= 2)
        def _():
            inv_copy.start()
            inv_copy.wait_send()
            child_copy.start()

    @pl.when(zhi == 0)
    def _():
        inverse_rows(inv, 0, n0, False)

        @pl.when(y >= 2)
        def _():
            landed(invx, x_recv.at[1])
            inverse_rows(invx, 1, n0 + 2, False)
            child_copy.start()

    scol = lax.rem(c, 16)

    def weight(h, i, j):
        hit = (cmap[h, r] == i * 16 + r) & (cmap[h, scol] == j * 32 + c)
        return jnp.where(hit, pattern[h * 16 + r, scol], 0).astype(F32)

    def base(i, j):
        return (
            front[i * 2 + j]
            + weight(zhi, i, j) * contrib[...]
            + weight(1 - zhi, i, j) * cpart[...]
        )

    def grp_rows(g):
        return pl.ds(pl.multiple_of(g * GRP, GRP), GRP)

    def pan_ref(k, g):
        return pan.at[grp_rows(g), pl.ds(pl.multiple_of(k * BLK, BLK), BLK)]

    def pan_copy(k, g, kind, to):
        part_ref = pan_ref(k, g)
        return remote(part_ref, part_ref, a_s.at[kind * 8 + g], a_recv.at[k * 8 + g], to)

    @pl.when(panel_dev)
    def _():
        landed(cpart, x_recv.at[0])
        for i in range(4):
            pan[pl.ds(i * BLK, BLK), pl.ds(pl.multiple_of(c * BLK, BLK), BLK)] = base(i, 0)

        landed(invx, x_recv.at[1])
        inverse_rows(invx, 1, n0 + 2, False)
        child_copy.start()

        def piece(p, carry):
            for k in range(4):
                @pl.when((k <= c) & (lax.rem(c, 2) * 8 + p != c))
                def _(k=k):
                    landed(
                        wbuf.at[pl.ds(pl.multiple_of(p * 32, 32), 32), pl.ds(k * BLK, BLK)],
                        w_recv.at[p * 4 + k],
                    )

            return carry

        lax.fori_loop(0, 8, piece, 0)
        for k in range(4):
            @pl.when(k <= c)
            def _(k=k):
                cols = pl.ds(k * BLK, BLK)
                hi, lo = split(wbuf[:, cols])
                wh[:, cols] = hi
                wl[:, cols] = lo

    def pass_panel(g):
        @pl.when(y == 0)
        def _():
            @pl.when(g >= AHEAD)
            def _():
                pan_copy(c, g - AHEAD, 0, y_up).wait_send()

            pan_copy(c, g, 0, y_up).start()

        @pl.when(core == 0)
        def _():
            pan_copy(c, g, 1, sib).start()

        for k in range(2):
            @pl.when((y == 1) & (core == k))
            def _(k=k):
                landed(pan_ref(k, g), a_recv.at[k * 8 + g])
                pan_copy(k, g, 2, sib).start()

    def make_factor(g):
        for n, waits in enumerate(((), (0,), (1,), (0, 2))):
            @pl.when(c == n)
            def _(n=n, waits=waits):
                for k in waits:
                    landed(pan_ref(k, g), a_recv.at[k * 8 + g])
                cols = pl.ds(0, (n + 1) * BLK)
                ah, al = split(pan[grp_rows(g), cols])
                w = wh[:, cols]
                fac[n, grp_rows(g)] = nt_dot(ah, w) + (nt_dot(ah, wl[:, cols]) + nt_dot(al, w))

    xs = 2 * lax.rem(y, 2) + core
    zs = y // 2
    dxs = lax.rem(x - xs + 4, 4)
    dz = jnp.abs(zlo - zs)
    c_dist = dz + jnp.where(dxs == 3, 1, dxs)
    c_go = (
        ((zlo >= zs) & (zlo < 3) & (dxs == 0), z_up),
        ((zlo <= zs) & (zlo > 0) & (dxs == 0), z_dn),
        ((dxs == 0) | ((core == 1) & (dxs == 1)), x_up),
        ((dxs == 0) | ((core == 0) & (dxs == 3)), x_dn),
    )

    def position(s):
        return lax.rem(8 - y, 8) if s == 0 else lax.rem(y + 7, 8)

    def lag(hops, s):
        return (hops * HOP_NUM) // HOP_DEN + s * R_OFF

    def ch_rows(m):
        return pl.ds(pl.multiple_of(m * CH, CH), CH)

    def fwd_to(s):
        return y_dn if s == 0 else y_up

    def rev_to(s):
        return y_up if s == 0 else y_dn

    def split_into(ref, hi_ref, lo_ref, rows, n):
        hi, lo = split(ref[...])
        cols = pl.ds(pl.multiple_of(n * BLK, BLK), BLK)
        hi_ref[rows, cols] = hi
        lo_ref[rows, cols] = lo

    def chunk_in(s, m, first, sends):
        own = 2 * s + core
        ref = fac.at[own, ch_rows(m)]
        sem = r_recv.at[own * NCH + m]
        if first is None:
            landed(ref, sem)
        else:
            pl.when(jnp.logical_not(first))(lambda: landed(ref, sem))
        for go, to, ss, before in sends:
            def start(to=to, ss=ss, before=before):
                if before is not None:
                    pl.when(m >= AHEAD)(remote(ref, ref, before, sem, to).wait_send)
                remote(ref, ref, ss, sem, to).start()

            pl.when(go)(start) if go is not None else start()
        split_into(ref, fh, fl, ch_rows(m), own)

    def sibling_in(s, m):
        n = 2 * s + 1 - core
        ref = fac.at[n, ch_rows(m)]
        landed(ref, r_recv.at[n * NCH + m])
        split_into(ref, fh, fl, ch_rows(m), n)

    def column_in(n, m):
        idx = m // (2 * PER_SLOT) * PER_SLOT + lax.rem(m, PER_SLOT)
        dst = facc.at[n, ch_rows(idx)]
        sem = c_recv.at[n * (NCH // 2) + idx]

        def go_on(src):
            for kind, (go, to) in enumerate(c_go):
                @pl.when(go)
                def _(kind=kind, to=to):
                    remote(src, dst, c_s.at[kind * 4 + n], sem, to).start()

            split_into(src, ch, cl, ch_rows(idx), n)

        @pl.when(c_dist == 0)
        def _():
            go_on(fac.at[n, ch_rows(m)])

        @pl.when(c_dist > 0)
        def _():
            landed(dst, sem)
            go_on(dst)

    def update(i, j):
        rows = pl.ds(pl.multiple_of(i * BLK, BLK), BLK)
        cr = pl.ds(j * BLK, BLK)
        u = nt_dot(fh[rows], ch[cr]) + (nt_dot(fh[rows], cl[cr]) + nt_dot(fl[rows], ch[cr]))
        on = ((i * 16 + r >= 4) & (j * 32 + c >= 4)).astype(jnp.int32).astype(F32)
        out[i * 2 + j] = base(i, j) - on * u

    def first_update(k):
        @pl.when((k == 0) & jnp.logical_not(panel_dev))
        def _():
            landed(cpart, x_recv.at[0])

        @pl.when(c >= 4)
        def _():
            update(k, 0)

        @pl.when(c < 4)
        def _():
            out[k * 2] = fac[jnp.minimum(c, 3), pl.ds(pl.multiple_of(k * BLK, BLK), BLK)]

    def within(m):
        return (m >= 0) & (m < NCH)

    def most(values):
        return functools.reduce(jnp.maximum, values)

    slack = jnp.where(c_dist > 0, C_SLACK, 0)

    def loop(half, lags, body):
        r_end = NCH + most([lags[k](1) for k in lags])
        c_end = most([lags[k](1 + c_dist) for k in lags]) + slack
        c0_end = PER_SLOT * (1 + half) + c_end
        end = NCH + c_end
        upd = jnp.maximum(r_end, c0_end)

        def step(t, carry):
            body(t)

            @pl.when((t >= upd) & (t < upd + 4))
            def _():
                first_update(t - upd)

            return carry

        lax.fori_loop(0, jnp.maximum(end, upd + 4), step, 0)

    @pl.when(zhi == 0)
    def _():
        pos = [position(0), position(1)]
        lags = {s: (lambda extra, s=s: lag(pos[s] + extra, s)) for s in (0, 1)}
        at = [[lags[s](e) for e in (0, 1)] + [lags[s](e + c_dist) + slack for e in (0, 1)] for s in (0, 1)]
        lead = y * R_OFF

        def body(t):
            g = t - lead

            @pl.when(panel_dev & within(t) & (lax.rem(t, PER_GRP) == 0))
            def _():
                pass_panel(t // PER_GRP)

            @pl.when(panel_dev & within(g) & (lax.rem(g, PER_GRP) == 0))
            def _():
                make_factor(g // PER_GRP)

            for s in (0, 1):
                m = t - at[s][0]

                @pl.when(within(m))
                def _(s=s, m=m):
                    q = 3 - lax.rem(m, 4)
                    chunk_in(s, m, pos[s] == 0, (
                        (pos[s] < 7, fwd_to(s), fwd_s.at[s * NCH + m],
                         fwd_s.at[s * NCH + jnp.maximum(m - AHEAD, 0)]),
                        (pos[s] == q, part, cross_s.at[s * 4 + q], None),
                        (None, sib, sib_s.at[s * 4 + q], None),
                    ))

                m1 = t - at[s][1]
                pl.when(within(m1))(functools.partial(sibling_in, s, m1))
                for e, n in ((0, 2 * s + core), (1, 2 * s + 1 - core)):
                    mc = t - at[s][2 + e]
                    pl.when(within(mc) & (lax.rem(mc // PER_SLOT, 2) == 0))(
                        functools.partial(column_in, n, mc)
                    )

        loop(0, lags, body)

    @pl.when(zhi == 1)
    def _():
        lags, at, info = {}, {}, {}
        for s in (0, 1):
            for q in range(4):
                d = lax.rem(position(s) - q + 8, 8)
                hops = q + 1 + jnp.where(d <= 4, d, 8 - d)
                lags[s, q] = lambda extra, s=s, hops=hops: lag(hops + extra, s)
                at[s, q] = [lags[s, q](e) for e in (0, 1)] + [
                    lags[s, q](e + c_dist) + slack for e in (0, 1)
                ]
                info[s, q] = (d <= 3, (d == 0) | (d >= 6))

        def body(t):
            for s in (0, 1):
                for q in range(4):
                    def mine(m, q=q):
                        return within(m) & (lax.rem(m + 16, 4) == 3 - q)

                    go_fwd, go_rev = info[s, q]
                    m = t - at[s, q][0]

                    @pl.when(mine(m))
                    def _(s=s, q=q, m=m, go_fwd=go_fwd, go_rev=go_rev):
                        chunk_in(s, m, None, (
                            (go_fwd, fwd_to(s), fwd_s.at[s * 4 + q], None),
                            (go_rev, rev_to(s), rev_s.at[s * 4 + q], None),
                            (None, sib, sib_s.at[s * 4 + q], None),
                        ))

                    m1 = t - at[s, q][1]
                    pl.when(mine(m1))(functools.partial(sibling_in, s, m1))
                    for e, n in ((0, 2 * s + core), (1, 2 * s + 1 - core)):
                        mc = t - at[s, q][2 + e]
                        pl.when(mine(mc) & (lax.rem(mc // PER_SLOT, 2) == 1))(
                            functools.partial(column_in, n, mc)
                        )

        loop(1, lags, body)

    def last_update(i, carry):
        update(i, 1)
        return carry

    lax.fori_loop(0, 4, last_update, 0)

    def left(ref, sem):
        remote(ref, ref, sem, sem, sib).wait_send()

    def sent(sq, carry):
        s, q = sq // 4, lax.rem(sq, 4)
        pos = jnp.where(s == 0, position(0), position(1))
        d = lax.rem(pos - q + 8, 8)
        quarter = fac.at[0, pl.ds(0, ROWS // 4)]

        @pl.when((zhi == 1) & (d <= 3))
        def _():
            left(quarter, fwd_s.at[sq])

        @pl.when((zhi == 0) & (pos < 7) & (q < AHEAD))
        def _():
            left(fac.at[0, ch_rows(0)], fwd_s.at[s * NCH + NCH - 1 - q])

        @pl.when((zhi == 1) & ((d == 0) | (d >= 6)))
        def _():
            left(quarter, rev_s.at[sq])

        @pl.when((zhi == 0) & (pos == q))
        def _():
            left(quarter, cross_s.at[sq])

        left(quarter, sib_s.at[sq])
        return carry

    lax.fori_loop(0, 8, sent, 0)
    for kind, (go, _to) in enumerate(c_go):
        for n in range(4):
            @pl.when(go)
            def _(kind=kind, n=n):
                left(facc.at[n], c_s.at[kind * 4 + n])

    child_copy.wait_send()

    @pl.when(zhi == 0)
    def _():
        inverse_rows(inv, 0, n0, True)
        inverse_rows(invx, 1, n0 + 2, True)

    @pl.when(panel_dev)
    def _():
        def one(g, carry):
            @pl.when((y == 0) & (g >= 8 - AHEAD))
            def _():
                pan_copy(c, g, 0, y_up).wait_send()

            @pl.when(core == 0)
            def _():
                pan_copy(c, g, 1, sib).wait_send()

            @pl.when(y == 1)
            def _():
                pan_copy(core, g, 2, sib).wait_send()

            return carry

        lax.fori_loop(0, 8, one, 0)


def body(front, contrib, child_map, pattern, inverse):
    vm = pl.BlockSpec(memory_space=pltpu.VMEM)
    sm = pl.BlockSpec(memory_space=pltpu.SMEM)
    dma = pltpu.SemaphoreType.DMA
    front_t = front.transpose(0, 2, 1, 3).reshape(8, BLK, BLK)
    out = pl.pallas_call(
        kernel,
        out_shape=jax.ShapeDtypeStruct((8, BLK, BLK), F32),
        in_specs=[vm, vm, sm, sm, vm],
        out_specs=vm,
        scratch_shapes=[
            pltpu.VMEM((4, ROWS, BLK), F32),
            pltpu.VMEM((4, ROWS // 2, BLK), F32),
            pltpu.VMEM((ROWS, 1024), F32),
            pltpu.VMEM((BLK, BLK), F32),
            pltpu.VMEM((32, 1024), F32),
            pltpu.VMEM((BLK, 1024), F32),
            pltpu.VMEM((BLK, 1024), BF16),
            pltpu.VMEM((BLK, 1024), BF16),
            pltpu.VMEM((ROWS, 1024), BF16),
            pltpu.VMEM((ROWS, 1024), BF16),
            pltpu.VMEM((ROWS // 2, 1024), BF16),
            pltpu.VMEM((ROWS // 2, 1024), BF16),
            dma((4 * NCH,)),
            dma((4 * NCH // 2,)),
            dma((32,)),
            dma((32,)),
            dma((2,)),
            dma((2 * NCH,)),
            dma((8,)),
            dma((8,)),
            dma((8,)),
            dma((16,)),
            dma((24,)),
            dma((8,)),
            dma((2,)),
        ],
        compiler_params=pltpu.CompilerParams(
            collective_id=0, has_side_effects=True, vmem_limit_bytes=48 << 20
        ),
        name="panel_step",
    )(front_t, contrib.reshape(BLK, BLK), child_map, pattern.reshape(32, 16), inverse)
    return out.reshape(4, 2, BLK, BLK).transpose(0, 2, 1, 3)


def solution(mesh):
    return jax.shard_map(
        body,
        mesh=mesh,
        in_specs=(
            P(None, "row", None, "col"),
            P(None, "row", None, "col"),
            P(),
            P(),
            P("col", None),
        ),
        out_specs=P(None, "row", None, "col"),
        check_vma=False,
    )
```

```python
import functools

import jax
import jax.numpy as jnp
from jax import lax
from jax.experimental import pallas as pl
from jax.experimental.pallas import tpu as pltpu
from jax.sharding import PartitionSpec as P

MESH = pl.DeviceIdType.MESH
F32 = jnp.float32
BF16 = jnp.bfloat16

BLK = 256
ROWS = 1024
CH = 64
NCH = ROWS // CH
PER_SLOT = BLK // CH
HOP_NUM, HOP_DEN = 3, 1
R_OFF = 1
GRP = 128
PER_GRP = GRP // CH
TAIL = 1024
C_SLACK = 0
AHEAD = 2


def nt_dot(a, b):
    return lax.dot_general(a, b, (((1,), (1,)), ((), ())), preferred_element_type=F32)


def split(x):
    hi = x.astype(BF16)
    return hi, (x - hi.astype(F32)).astype(BF16)


def kernel(
    front, contrib, cmap, pattern, inv, out,
    fac, facc, pan, cpart, invx, wbuf, wh, wl, fh, fl, ch, cl,
    r_recv, c_recv, a_recv, w_recv, x_recv,
    fwd_s, rev_s, cross_s, sib_s, c_s, h_s, a_s, w_s, x_s,
):
    r = lax.axis_index("row")
    c = lax.axis_index("col")
    x, zlo = lax.rem(r, 4), r // 4
    zhi, y, core = c // 16, lax.rem(c // 2, 8), lax.rem(c, 2)
    n0 = lax.rem(c, 16) // 8

    def dev(x_, zlo_, zhi_, y_, core_):
        return (zlo_ * 4 + x_, zhi_ * 16 + y_ * 2 + core_)

    y_up = dev(x, zlo, zhi, lax.rem(y + 1, 8), core)
    y_dn = dev(x, zlo, zhi, lax.rem(y + 7, 8), core)
    sib = dev(x, zlo, zhi, y, 1 - core)
    part = dev(x, zlo, 1 - zhi, y, core)
    mirror = dev(x, 3 - zlo, 1 - zhi, y, core)
    x_up = dev(lax.rem(x + 1, 4), zlo, zhi, y, core)
    x_dn = dev(lax.rem(x + 3, 4), zlo, zhi, y, core)
    z_up = dev(x, jnp.minimum(zlo + 1, 3), zhi, y, core)
    z_dn = dev(x, jnp.maximum(zlo - 1, 0), zhi, y, core)
    across = tuple((to[0], to[1] + 1 - 2 * core) for to in (z_up, z_dn, x_up, x_dn))
    panel_dev = (zhi == 0) & (y < 2)

    def remote(src, dst, ss, rs, to):
        return pltpu.make_async_remote_copy(
            src_ref=src, dst_ref=dst, send_sem=ss, recv_sem=rs, device_id=to, device_id_type=MESH
        )

    def landed(ref, sem):
        pltpu.make_async_copy(ref, ref, sem).wait()

    bar = pltpu.get_barrier_semaphore()

    def greet(to):
        pl.semaphore_signal(bar, inc=1, device_id=to, device_id_type=MESH)

    for to in (y_up, y_dn, sib, part, mirror, x_up, x_dn) + across[2:]:
        greet(to)

    @pl.when(zlo < 3)
    def _():
        greet(z_up)
        greet(across[0])

    @pl.when(zlo > 0)
    def _():
        greet(z_dn)
        greet(across[1])

    @pl.when(panel_dev)
    def _():
        def one(p, carry):
            peer = lax.rem(c, 2) * 8 + p

            @pl.when(peer != c)
            def _():
                greet((r, peer))

            return carry

        lax.fori_loop(0, 8, one, 0)

    expect = 9 + 2 * (zlo < 3).astype(jnp.int32) + 2 * (zlo > 0).astype(jnp.int32)
    from_panel = (n0 != c).astype(jnp.int32) + (n0 + 2 != c).astype(jnp.int32)
    expect = expect + jnp.where(zhi == 0, from_panel, 0)
    pl.semaphore_wait(bar, expect)

    child_copy = remote(contrib, cpart, x_s.at[0], x_recv.at[0], part)
    inv_copy = remote(inv, invx, x_s.at[1], x_recv.at[1], mirror)
    wrow = pl.ds(pl.multiple_of(lax.rem(c, 8) * 32, 32), 32)
    wslot = lax.rem(c, 8)

    def inverse_rows(src, which, owner, wait):
        for k in range(4):
            cols = pl.ds(k * BLK, BLK)

            @pl.when(k <= owner)
            def _(k=k, cols=cols):
                @pl.when(owner == c)
                def _():
                    if not wait:
                        wbuf[wrow, cols] = src[:, cols]

                @pl.when(owner != c)
                def _():
                    cp = remote(
                        src.at[:, cols], wbuf.at[wrow, cols],
                        w_s.at[which * 4 + k], w_recv.at[wslot * 4 + k], (r, owner),
                    )
                    if wait:
                        cp.wait_send()
                    else:
                        cp.start()

    @pl.when(zhi == 1)
    def _():
        @pl.when(y < 2)
        def _():
            child_copy.start()
            inv_copy.start()
            inv_copy.wait_send()

        @pl.when(y >= 2)
        def _():
            inv_copy.start()
            inv_copy.wait_send()
            child_copy.start()

    @pl.when(zhi == 0)
    def _():
        inverse_rows(inv, 0, n0, False)

        @pl.when(y >= 2)
        def _():
            landed(invx, x_recv.at[1])
            inverse_rows(invx, 1, n0 + 2, False)
            child_copy.start()

    scol = lax.rem(c, 16)

    def weight(h, i, j):
        hit = (cmap[h, r] == i * 16 + r) & (cmap[h, scol] == j * 32 + c)
        return jnp.where(hit, pattern[h * 16 + r, scol], 0).astype(F32)

    def base(i, j):
        return (
            front[i * 2 + j]
            + weight(zhi, i, j) * contrib[...]
            + weight(1 - zhi, i, j) * cpart[...]
        )

    def grp_rows(g):
        return pl.ds(pl.multiple_of(g * GRP, GRP), GRP)

    def pan_ref(k, g):
        return pan.at[grp_rows(g), pl.ds(pl.multiple_of(k * BLK, BLK), BLK)]

    def pan_copy(k, g, kind, to):
        part_ref = pan_ref(k, g)
        return remote(part_ref, part_ref, a_s.at[kind * 8 + g], a_recv.at[k * 8 + g], to)

    @pl.when(panel_dev)
    def _():
        landed(cpart, x_recv.at[0])
        for i in range(4):
            pan[pl.ds(i * BLK, BLK), pl.ds(pl.multiple_of(c * BLK, BLK), BLK)] = base(i, 0)

        landed(invx, x_recv.at[1])
        inverse_rows(invx, 1, n0 + 2, False)
        child_copy.start()

        def piece(p, carry):
            for k in range(4):
                @pl.when((k <= c) & (lax.rem(c, 2) * 8 + p != c))
                def _(k=k):
                    landed(
                        wbuf.at[pl.ds(pl.multiple_of(p * 32, 32), 32), pl.ds(k * BLK, BLK)],
                        w_recv.at[p * 4 + k],
                    )

            return carry

        lax.fori_loop(0, 8, piece, 0)
        for k in range(4):
            @pl.when(k <= c)
            def _(k=k):
                cols = pl.ds(k * BLK, BLK)
                hi, lo = split(wbuf[:, cols])
                wh[:, cols] = hi
                wl[:, cols] = lo

    def pass_panel(g):
        @pl.when(y == 0)
        def _():
            @pl.when(g >= AHEAD)
            def _():
                pan_copy(c, g - AHEAD, 0, y_up).wait_send()

            pan_copy(c, g, 0, y_up).start()

        @pl.when(core == 0)
        def _():
            pan_copy(c, g, 1, sib).start()

        for k in range(2):
            @pl.when((y == 1) & (core == k))
            def _(k=k):
                landed(pan_ref(k, g), a_recv.at[k * 8 + g])
                pan_copy(k, g, 2, sib).start()

    def make_factor(g):
        for n, waits in enumerate(((), (0,), (1,), (0, 2))):
            @pl.when(c == n)
            def _(n=n, waits=waits):
                for k in waits:
                    landed(pan_ref(k, g), a_recv.at[k * 8 + g])
                cols = pl.ds(0, (n + 1) * BLK)
                ah, al = split(pan[grp_rows(g), cols])
                w = wh[:, cols]
                fac[n, grp_rows(g)] = nt_dot(ah, w) + (nt_dot(ah, wl[:, cols]) + nt_dot(al, w))

    xs = 2 * lax.rem(y, 2) + core
    zs = y // 2
    dxs = lax.rem(x - xs + 4, 4)
    dz = jnp.abs(zlo - zs)
    c_dist = dz + jnp.where(dxs == 3, 1, dxs)
    c_go = (
        ((zlo >= zs) & (zlo < 3) & (dxs == 0), z_up),
        ((zlo <= zs) & (zlo > 0) & (dxs == 0), z_dn),
        ((dxs == 0) | ((core == 1) & (dxs == 1)), x_up),
        ((dxs == 0) | ((core == 0) & (dxs == 3)), x_dn),
    )

    helps = (zlo == zs) & (x == 2 * lax.rem(y, 2) + 1 - core)
    help_go = (zlo < 3, zlo > 0, None, None)

    def position(s):
        return lax.rem(8 - y, 8) if s == 0 else lax.rem(y + 7, 8)

    def lag(hops, s):
        return (hops * HOP_NUM) // HOP_DEN + s * R_OFF

    def ch_rows(m):
        return pl.ds(pl.multiple_of(m * CH, CH), CH)

    def fwd_to(s):
        return y_dn if s == 0 else y_up

    def rev_to(s):
        return y_up if s == 0 else y_dn

    def split_into(ref, hi_ref, lo_ref, rows, n):
        hi, lo = split(ref[...])
        cols = pl.ds(pl.multiple_of(n * BLK, BLK), BLK)
        hi_ref[rows, cols] = hi
        lo_ref[rows, cols] = lo

    def chunk_in(s, m, first, sends):
        own = 2 * s + core
        ref = fac.at[own, ch_rows(m)]
        sem = r_recv.at[own * NCH + m]
        if first is None:
            landed(ref, sem)
        else:
            pl.when(jnp.logical_not(first))(lambda: landed(ref, sem))
        for go, to, ss, before in sends:
            def start(to=to, ss=ss, before=before):
                if before is not None:
                    pl.when(m >= AHEAD)(remote(ref, ref, before, sem, to).wait_send)
                remote(ref, ref, ss, sem, to).start()

            pl.when(go)(start) if go is not None else start()
        split_into(ref, fh, fl, ch_rows(m), own)

    def col_index(m):
        return (m & (2 * PER_SLOT)) // 2 + (m & (PER_SLOT - 1))

    def help_out(s, m):
        n, idx = 2 * s + core, col_index(m)
        for kind, (go, to) in enumerate(zip(help_go, across)):
            def start(kind=kind, to=to):
                remote(
                    fac.at[n, ch_rows(m)], facc.at[n, ch_rows(idx)],
                    h_s.at[kind * 2 + s], c_recv.at[n * (NCH // 2) + idx], to,
                ).start()

            start() if go is None else pl.when(go)(start)

    def sibling_in(s, m):
        n = 2 * s + 1 - core
        ref = fac.at[n, ch_rows(m)]
        landed(ref, r_recv.at[n * NCH + m])
        split_into(ref, fh, fl, ch_rows(m), n)

    def column_in(n, m, own):
        idx = col_index(m)
        dst = facc.at[n, ch_rows(idx)]
        sem = c_recv.at[n * (NCH // 2) + idx]

        def go_on(src, send):
            for kind, (go, to) in enumerate(c_go if send else ()):
                @pl.when(go)
                def _(kind=kind, to=to):
                    remote(src, dst, c_s.at[kind * 4 + n], sem, to).start()

            split_into(src, ch, cl, ch_rows(idx), n)

        @pl.when(c_dist == 0)
        def _():
            go_on(fac.at[n, ch_rows(m)], own)

        @pl.when(c_dist > 0)
        def _():
            landed(dst, sem)
            go_on(dst, True)

    def update(i, j):
        rows = pl.ds(pl.multiple_of(i * BLK, BLK), BLK)
        cr = pl.ds(j * BLK, BLK)
        u = nt_dot(fh[rows], ch[cr]) + (nt_dot(fh[rows], cl[cr]) + nt_dot(fl[rows], ch[cr]))
        on = ((i * 16 + r >= 4) & (j * 32 + c >= 4)).astype(jnp.int32).astype(F32)
        out[i * 2 + j] = base(i, j) - on * u

    def first_update(k):
        @pl.when((k == 0) & jnp.logical_not(panel_dev))
        def _():
            landed(cpart, x_recv.at[0])

        @pl.when(c >= 4)
        def _():
            update(k, 0)

        @pl.when(c < 4)
        def _():
            out[k * 2] = fac[jnp.minimum(c, 3), pl.ds(pl.multiple_of(k * BLK, BLK), BLK)]

    def within(m):
        return (m & -NCH) == 0

    def most(values):
        return functools.reduce(jnp.maximum, values)

    slack = jnp.where(c_dist > 0, C_SLACK, 0)

    def loop(half, lags, body):
        r_end = NCH + most([lags[k](1) for k in lags])
        c_end = most([lags[k](jnp.maximum(c_dist, 1)) for k in lags]) + slack
        c0_end = PER_SLOT * (1 + half) + c_end
        end = NCH + c_end
        upd = jnp.maximum(r_end, c0_end)

        def step(t, carry):
            body(t)

            @pl.when(((t - upd) & -4) == 0)
            def _():
                first_update(t - upd)

            return carry

        lax.fori_loop(0, jnp.maximum(end, upd + 4), step, 0)

    @pl.when(zhi == 0)
    def _():
        pos = [position(0), position(1)]
        lags = {s: (lambda extra, s=s: lag(pos[s] + extra, s)) for s in (0, 1)}
        at = [[lags[s](e) for e in (0, 1)] + [lags[s](jnp.maximum(c_dist, e)) + slack for e in (0, 1)] for s in (0, 1)]
        lead = y * R_OFF

        def body(t):
            g = t - lead

            @pl.when(panel_dev & within(t) & ((t & (PER_GRP - 1)) == 0))
            def _():
                pass_panel(t // PER_GRP)

            @pl.when(panel_dev & within(g) & ((g & (PER_GRP - 1)) == 0))
            def _():
                make_factor(g // PER_GRP)

            for s in (0, 1):
                m = t - at[s][0]

                @pl.when(within(m))
                def _(s=s, m=m):
                    q = 3 - (m & 3)
                    chunk_in(s, m, pos[s] == 0, (
                        (pos[s] < 7, fwd_to(s), fwd_s.at[s * NCH + m],
                         fwd_s.at[s * NCH + jnp.maximum(m - AHEAD, 0)]),
                        (pos[s] == q, part, cross_s.at[s * 4 + q], None),
                        (None, sib, sib_s.at[s * 4 + q], None),
                    ))
                    pl.when(helps & ((m & PER_SLOT) == 0))(
                        functools.partial(help_out, s, m)
                    )

                m1 = t - at[s][1]
                pl.when(within(m1))(functools.partial(sibling_in, s, m1))
                for e, n in ((0, 2 * s + core), (1, 2 * s + 1 - core)):
                    mc = t - at[s][2 + e]
                    pl.when((mc & -(2 * BLK // CH + PER_SLOT)) == 0)(
                        functools.partial(column_in, n, mc, e == 0)
                    )

        loop(0, lags, body)

    @pl.when(zhi == 1)
    def _():
        lags, at, info = {}, {}, {}
        for s in (0, 1):
            for q in range(4):
                d = lax.rem(position(s) - q + 8, 8)
                hops = q + 1 + jnp.where(d <= 4, d, 8 - d)
                lags[s, q] = lambda extra, s=s, hops=hops: lag(hops + extra, s)
                at[s, q] = [lags[s, q](e) + 3 - q for e in (0, 1)] + [
                    lags[s, q](jnp.maximum(c_dist, e)) + slack + 3 - q for e in (0, 1)
                ]
                info[s, q] = (d <= 3, (d == 0) | (d >= 6))

        def body(t):
            for s in (0, 1):
                for q in range(4):
                    go_fwd, go_rev = info[s, q]
                    k = 3 - q
                    m = t - at[s, q][0]

                    @pl.when((m & -13) == 0)
                    def _(s=s, q=q, m=m + k, go_fwd=go_fwd, go_rev=go_rev):
                        chunk_in(s, m, None, (
                            (go_fwd, fwd_to(s), fwd_s.at[s * 4 + q], None),
                            (go_rev, rev_to(s), rev_s.at[s * 4 + q], None),
                            (None, sib, sib_s.at[s * 4 + q], None),
                        ))
                        pl.when(helps & ((m & PER_SLOT) != 0))(functools.partial(help_out, s, m))

                    m1 = t - at[s, q][1]
                    pl.when((m1 & -13) == 0)(functools.partial(sibling_in, s, m1 + k))
                    for e, n in ((0, 2 * s + core), (1, 2 * s + 1 - core)):
                        mc = t - at[s, q][2 + e]
                        pl.when((mc & -9) == 4)(functools.partial(column_in, n, mc + k, e == 0))

        loop(1, lags, body)

    def last_update(k, carry):
        rows = pl.ds(pl.multiple_of(k * TAIL, TAIL), TAIL)
        cr = pl.ds(BLK, BLK)
        u = nt_dot(fh[rows], ch[cr]) + (nt_dot(fh[rows], cl[cr]) + nt_dot(fl[rows], ch[cr]))
        for p in range(TAIL // BLK):
            i = k * (TAIL // BLK) + p
            on = (i * 16 + r >= 4).astype(jnp.int32).astype(F32)
            out[i * 2 + 1] = base(i, 1) - on * u[p * BLK : (p + 1) * BLK]
        return carry

    lax.fori_loop(0, ROWS // TAIL, last_update, 0)

    def left(ref, sem):
        remote(ref, ref, sem, sem, sib).wait_send()

    def sent(sq, carry):
        s, q = sq // 4, lax.rem(sq, 4)
        pos = jnp.where(s == 0, position(0), position(1))
        d = lax.rem(pos - q + 8, 8)
        quarter = fac.at[0, pl.ds(0, ROWS // 4)]

        @pl.when((zhi == 1) & (d <= 3))
        def _():
            left(quarter, fwd_s.at[sq])

        @pl.when((zhi == 0) & (pos < 7) & (q < AHEAD))
        def _():
            left(fac.at[0, ch_rows(0)], fwd_s.at[s * NCH + NCH - 1 - q])

        @pl.when((zhi == 1) & ((d == 0) | (d >= 6)))
        def _():
            left(quarter, rev_s.at[sq])

        @pl.when((zhi == 0) & (pos == q))
        def _():
            left(quarter, cross_s.at[sq])

        left(quarter, sib_s.at[sq])
        return carry

    lax.fori_loop(0, 8, sent, 0)
    for kind, (go, _to) in enumerate(c_go):
        for n in range(4):
            @pl.when(go & ((c_dist > 0) | (core == n % 2)))
            def _(kind=kind, n=n):
                left(facc.at[n], c_s.at[kind * 4 + n])

    for kind, go in enumerate(help_go):
        for n in range(2):
            @pl.when(helps if go is None else helps & go)
            def _(kind=kind, n=n):
                left(facc.at[n], h_s.at[kind * 2 + n])

    child_copy.wait_send()

    @pl.when(zhi == 0)
    def _():
        inverse_rows(inv, 0, n0, True)
        inverse_rows(invx, 1, n0 + 2, True)

    @pl.when(panel_dev)
    def _():
        def one(g, carry):
            @pl.when((y == 0) & (g >= 8 - AHEAD))
            def _():
                pan_copy(c, g, 0, y_up).wait_send()

            @pl.when(core == 0)
            def _():
                pan_copy(c, g, 1, sib).wait_send()

            @pl.when(y == 1)
            def _():
                pan_copy(core, g, 2, sib).wait_send()

            return carry

        lax.fori_loop(0, 8, one, 0)


def body(front, contrib, child_map, pattern, inverse):
    vm = pl.BlockSpec(memory_space=pltpu.VMEM)
    sm = pl.BlockSpec(memory_space=pltpu.SMEM)
    dma = pltpu.SemaphoreType.DMA
    front_t = front.transpose(0, 2, 1, 3).reshape(8, BLK, BLK)
    out = pl.pallas_call(
        kernel,
        out_shape=jax.ShapeDtypeStruct((8, BLK, BLK), F32),
        in_specs=[vm, vm, sm, sm, vm],
        out_specs=vm,
        scratch_shapes=[
            pltpu.VMEM((4, ROWS, BLK), F32),
            pltpu.VMEM((4, ROWS // 2, BLK), F32),
            pltpu.VMEM((ROWS, 1024), F32),
            pltpu.VMEM((BLK, BLK), F32),
            pltpu.VMEM((32, 1024), F32),
            pltpu.VMEM((BLK, 1024), F32),
            pltpu.VMEM((BLK, 1024), BF16),
            pltpu.VMEM((BLK, 1024), BF16),
            pltpu.VMEM((ROWS, 1024), BF16),
            pltpu.VMEM((ROWS, 1024), BF16),
            pltpu.VMEM((ROWS // 2, 1024), BF16),
            pltpu.VMEM((ROWS // 2, 1024), BF16),
            dma((4 * NCH,)),
            dma((4 * NCH // 2,)),
            dma((32,)),
            dma((32,)),
            dma((2,)),
            dma((2 * NCH,)),
            dma((8,)),
            dma((8,)),
            dma((8,)),
            dma((16,)),
            dma((8,)),
            dma((24,)),
            dma((8,)),
            dma((2,)),
        ],
        compiler_params=pltpu.CompilerParams(
            collective_id=0, has_side_effects=True, vmem_limit_bytes=48 << 20
        ),
        name="panel_step",
    )(front_t, contrib.reshape(BLK, BLK), child_map, pattern.reshape(32, 16), inverse)
    return out.reshape(4, 2, BLK, BLK).transpose(0, 2, 1, 3)


def solution(mesh):
    return jax.shard_map(
        body,
        mesh=mesh,
        in_specs=(
            P(None, "row", None, "col"),
            P(None, "row", None, "col"),
            P(),
            P(),
            P("col", None),
        ),
        out_specs=P(None, "row", None, "col"),
        check_vma=False,
    )
```
